32 devices in a mesh: leaf: 16 (over z, y, x), head: 2 (over core).
Axes of the slice: x: 2, y: 2, z: 4, core: 2. Of those that a mesh axis runs over, the one named last changes fastest.
Arguments:
- cand_owner: int32 [128, 500, 1], P('leaf'), may hold values from 0 to 15; in each aligned block of 4000 rows (0 to 3999, 4000 to 7999, ..., all dimensions but the last counted through in order) at most 500 rows name the same one
- cand_row: int32 [128, 500], P('leaf'), may hold values from 0 to 2047
- table: bfloat16 [32768, 1024], P('leaf', 'head'), may hold values from -6 to 6
- position: bfloat16 [500, 1024], P(None, 'head'), may hold values from -3 to 3
- w_query: bfloat16 [1024, 1024], P(None, 'head'), may hold values from -0.375 to 0.375
- w_key: bfloat16 [1024, 1024], P(None, 'head'), may hold values from -0.375 to 0.375
- w_value: bfloat16 [1024, 1024], P(None, 'head'), may hold values from -0.1875 to 0.1875
- w_out: bfloat16 [1024, 1024], P('head'), may hold values from -0.1875 to 0.1875
- gain: float32 [1024], P('head'), may hold values from 0.1 to 1.9
- shift_bias: float32 [1024], P('head'), may hold values from -3 to 3
Outputs:
- reranked: bfloat16 [128, 500, 1024], P('leaf', None, 'head')
The draws below stay inside these ranges and needn't reach their ends.
Inputs may be any that keep to these rules, and one draw needn't show every extreme that they name: `cand_owner`: among the 4000 candidates of the lists of one index of leaf, no subtree is named more than 500 times, a bound that some block reaches.
All inputs are finite; a program needn't handle non-finite values.
Results may differ from the reference program's by a relative error of at most 0.012.
Values may be sent and summed in bfloat16 or wider, within the bound.
A program may use at most 128 MiB of HBM per device.

```python
import math
import jax
import jax.numpy as jnp
import numpy as np
from jax import lax

D = 1024
HEADS = 16
HEAD_DIM = 64
L = 500
U_DEV = 8
ROWS_DEV = 2048
SUBTREES = 16
USERS = 128
ROWS = 32768
CAP = 500


def set_ends(drawn, stream_key, low, high):
    extent = drawn.shape
    place = [jax.random.randint(jax.random.fold_in(stream_key, axis), (), 0, extent[axis]) for axis in range(len(extent))]
    drawn = drawn.at[tuple(place)].set(low)
    longest = extent.index(max(extent))
    place[longest] = (place[longest] + 1) % extent[longest]
    return drawn.at[tuple(place)].set(high)


def steps_of(stream_key, shape, cuts, least, top_value):
    level, own = 1.0, jax.random.fold_in(stream_key, 6)
    for dim, blocks in cuts:
        steps = jnp.exp(jax.random.uniform(jax.random.fold_in(own, dim), (blocks,), jnp.float32, least / len(cuts), top_value / len(cuts)))
        level = level * jnp.repeat(steps, shape[dim] // blocks).reshape([-1 if axis == dim else 1 for axis in range(len(shape))])
    return level


def deal_out(own_key, own, number, rows, amount, top, bound, slope):
    ranking = jax.random.permutation(own_key, amount)
    heavy_load, ordinary = portions_of(amount, rows * top, bound, slope, True), portions_of(amount, rows * top, bound, slope, False)
    places = jnp.arange(amount)

    def named(lengths, rotation):
        used = int((lengths > 0).sum())
        fixed = max(1, used // 4)
        passed = fixed + (places - fixed + rotation * (used - fixed)) % max(1, amount - fixed)
        return jnp.zeros((amount,), jnp.int32).at[ranking[jnp.where(places < fixed, places, passed)]].set(jnp.asarray(lengths, jnp.int32))

    lengths = jnp.where(number % 4 == 0, named(heavy_load, number // 4), named(ordinary, number - number // 4 - 1))
    mixed = jax.random.permutation(jax.random.fold_in(own, 3), amount)
    source_of, sink = mixed[0:amount // 2 * 2:2], mixed[1:amount // 2 * 2:2]
    margin = jnp.minimum(lengths[source_of] - 1, bound - lengths[sink]) // 2
    margin = jnp.where((source_of == ranking[0]) | (sink == ranking[0]) | (lengths[sink] == 0), 0, jnp.maximum(margin, 0))
    passed = jax.random.randint(jax.random.fold_in(own, 4), (amount // 2,), 0, 1 << 20) % (margin + 1)
    lengths = lengths.at[source_of].add(-passed).at[sink].add(passed)
    labels = jnp.searchsorted(jnp.cumsum(lengths), jnp.arange(rows * top), side="right").astype(jnp.int32)
    grid = labels.reshape(top, rows).T
    grid = grid[jax.random.permutation(jax.random.fold_in(own, 1), rows)]
    rotation = jax.random.randint(jax.random.fold_in(own, 2), (rows, 1), 0, top)
    return jnp.take_along_axis(grid, (jnp.arange(top)[None, :] + rotation) % top, axis=1)


def portions_of(number_of, total, most, lean, full):
    portions = [(1 << 20) // math.isqrt(rank ** lean) + 1 for rank in range(1, number_of + 1)]
    largest = most if full else min(most, max(-(-total // number_of), total * portions[0] // sum(portions)))
    least = 1 if total - largest >= number_of - 1 else 0
    counts, spare = [largest] + [least] * (number_of - 1), total - largest - least * (number_of - 1)
    while spare > 0:
        candidates = [i for i in range(1, number_of) if counts[i] < largest] or [i for i in range(1, number_of) if counts[i] < most]
        whole, left = sum([portions[i] for i in candidates]), spare
        for i in candidates:
            more = min(most - counts[i], max(1, left * portions[i] // whole), spare)
            counts[i] = counts[i] + more
            spare = spare - more
    return np.array(counts)


def centred(key, dims, width, bound, split=(), held_as=jnp.bfloat16):
    factor_of = steps_of(key, dims, split, -0.22, 0.18) if split else 1.0
    entries = jax.random.normal(key, dims, jnp.float32) * width * factor_of
    return jnp.minimum(jnp.maximum(entries, -bound), bound).astype(held_as)


def setup_inputs(seed: int = 0) -> dict:
    seeds = jax.random.split(jax.random.key(seed), 11)
    cand_owner_keys = jax.random.split(jax.random.fold_in(seeds[0], 1), USERS * L // (U_DEV * L))
    cand_owner_turns = jax.random.permutation(jax.random.fold_in(seeds[0], 3), USERS * L // (U_DEV * L))
    cand_owner = jax.vmap(lambda own, number: deal_out(jax.random.fold_in(seeds[0], 2), own, number, U_DEV * L, SUBTREES, 1, CAP, 2))(cand_owner_keys, cand_owner_turns).reshape((USERS, L, 1))
    cand_row = set_ends(jax.random.randint(seeds[1], (USERS, L), 0, ROWS_DEV), jax.random.fold_in(seeds[1], 1), 0, ROWS_DEV - 1).astype(jnp.int32)
    table = centred(seeds[2], (ROWS, D), 1.0, 6.0, ((0, 16), (1, 2)))
    position = centred(seeds[3], (L, D), 0.5, 3.0, ((1, 2),))
    w_query = centred(seeds[4], (D, D), (D // 4) ** -0.5, 0.375, ((1, 2),))
    w_key = centred(seeds[5], (D, D), (D // 4) ** -0.5, 0.375, ((1, 2),))
    w_value = centred(seeds[6], (D, D), D ** -0.5, 0.1875, ((1, 2),))
    w_out = centred(seeds[7], (D, D), D ** -0.5, 0.1875, ((0, 2),))
    gain = jnp.clip(1.0 + 0.18 * jax.random.normal(seeds[8], (D,), jnp.float32), 0.1, 1.9)
    shift_bias = centred(seeds[9], (D,), 0.5, 3.0, ((0, 2),), jnp.float32)
    return {"cand_owner": cand_owner, "cand_row": cand_row, "table": table, "position": position, "w_query": w_query, "w_key": w_key, "w_value": w_value, "w_out": w_out, "gain": gain, "shift_bias": shift_bias}


def reference(cand_owner, cand_row, table, position, w_query, w_key, w_value, w_out, gain, shift_bias):
    item = (cand_owner[:, :, 0] * ROWS_DEV + cand_row).astype(jnp.int32)
    scale = 1.0 / HEAD_DIM ** 0.5

    def one_user(ids):
        embedded = jnp.take(table, ids, axis=0)
        x = (embedded.astype(jnp.float32) + position.astype(jnp.float32)).astype(jnp.bfloat16)
        q = jnp.dot(x, w_query, preferred_element_type=jnp.float32).astype(jnp.bfloat16)
        k = jnp.dot(x, w_key, preferred_element_type=jnp.float32).astype(jnp.bfloat16)
        v = jnp.dot(x, w_value, preferred_element_type=jnp.float32).astype(jnp.bfloat16)
        q = q.reshape(L, HEADS, HEAD_DIM).astype(jnp.float32)
        k = k.reshape(L, HEADS, HEAD_DIM).astype(jnp.float32)
        v = v.reshape(L, HEADS, HEAD_DIM).astype(jnp.float32)
        scores = jnp.einsum('qhd,khd->hqk', q, k) * scale
        weights = jax.nn.softmax(scores, axis=-1).astype(jnp.bfloat16)
        context = jnp.einsum('hqk,khd->qhd', weights.astype(jnp.float32), v).astype(jnp.bfloat16).reshape(L, D)
        y = x.astype(jnp.float32) + jnp.dot(context, w_out, preferred_element_type=jnp.float32)
        mean = lax.optimization_barrier(jnp.mean(y, axis=1, keepdims=True))
        var = lax.optimization_barrier(jnp.mean(y * y, axis=1, keepdims=True)) - mean * mean
        normed = (y - mean) * lax.rsqrt(var + 1e-05) * gain[None, :] + shift_bias[None, :]
        return normed.astype(jnp.bfloat16)
    return lax.map(one_user, item)
```

```python
import functools
import math

import jax
import jax.numpy as jnp
from jax import lax
from jax.experimental import pallas as pl
from jax.experimental.pallas import tpu as pltpu
from jax.sharding import PartitionSpec as P

HEAD_DIM = 64
PAIR = 2 * HEAD_DIM
SPLIT = 2


def mm(a, b):
    return jnp.dot(a, b, preferred_element_type=jnp.float32)


def attend_kernel(length, xo_ref, xt_ref, qo, qt, ko, kt, vo, vt, ctx_ref):
    xo, xt = xo_ref[0], xt_ref[0]
    padded, cols = xo.shape
    scale = math.log2(math.e) / HEAD_DIM**0.5
    q = ((mm(xo, qo[...]) + mm(xt, qt[...])) * scale).astype(jnp.bfloat16)
    k = (mm(xo, ko[...]) + mm(xt, kt[...])).astype(jnp.bfloat16)
    v = (mm(xo, vo[...]) + mm(xt, vt[...])).astype(jnp.bfloat16)
    low = lax.broadcasted_iota(jnp.int32, (padded, PAIR), 1) < HEAD_DIM
    real = lax.broadcasted_iota(jnp.int32, (padded, PAIR), 0) < length
    ones = jnp.where(real, 1.0, 0.0).astype(jnp.bfloat16)
    for pair in range(cols // PAIR):
        lanes = slice(pair * PAIR, (pair + 1) * PAIR)
        qp, kp, vp = q[:, lanes], k[:, lanes], v[:, lanes]
        vx = jnp.concatenate([jnp.where(real, vp, jnp.zeros_like(vp)), ones], axis=1)
        halves = []
        for mask in (low, jnp.logical_not(low)):
            qm = jnp.where(mask, qp, jnp.zeros_like(qp))
            s = lax.dot_general(
                qm, kp, (((1,), (1,)), ((), ())), preferred_element_type=jnp.float32
            )
            e = jnp.exp2(s - jnp.max(s, axis=1, keepdims=True)).astype(jnp.bfloat16)
            o = mm(e, vx)
            halves.append(o[:, :PAIR] / o[:, PAIR:])
        ctx_ref[0, :, lanes] = jnp.where(low, halves[0], halves[1]).astype(jnp.bfloat16)


def attend(length, xo, xt, weights):
    users, padded, cols = xo.shape
    block = pl.BlockSpec((1, padded, cols), lambda u: (u, 0, 0))
    whole = pl.BlockSpec((cols, cols), lambda u: (0, 0))
    flops = users * (12 * padded * cols * cols + 8 * padded * padded * cols)
    return pl.pallas_call(
        functools.partial(attend_kernel, length),
        grid=(users,),
        out_shape=jax.ShapeDtypeStruct(xo.shape, jnp.bfloat16),
        in_specs=[block, block] + [whole] * 6,
        out_specs=block,
        compiler_params=pltpu.CompilerParams(vmem_limit_bytes=44 * 1024 * 1024),
        cost_estimate=pl.CostEstimate(
            flops=flops,
            bytes_accessed=3 * xo.size * 2 + 12 * cols * cols,
            transcendentals=users * (cols // HEAD_DIM) * padded * padded,
        ),
        name="attend",
    )(xo, xt, *weights)


def finish_kernel(length, xo_ref, xt_ref, co_ref, ct_ref, oo, to, ot, tt, gain, bias, out_ref):
    co, ct = co_ref[0], ct_ref[0]
    yo = xo_ref[0].astype(jnp.float32) + mm(co, oo[...]) + mm(ct, to[...])
    yt = xt_ref[0].astype(jnp.float32) + mm(co, ot[...]) + mm(ct, tt[...])
    width = 2 * yo.shape[1]
    mean = jnp.sum(yo + yt, axis=1, keepdims=True) / width
    var = jnp.sum(yo * yo + yt * yt, axis=1, keepdims=True) / width - mean * mean
    normed = (yo - mean) * lax.rsqrt(var + 1e-05) * gain[...] + bias[...]
    out_ref[0] = normed[:length].astype(jnp.bfloat16)


def finish(length, xo, xt, co, ct, weights, gain, bias):
    users, padded, cols = xo.shape
    block = pl.BlockSpec((1, padded, cols), lambda u: (u, 0, 0))
    whole = pl.BlockSpec((cols, cols), lambda u: (0, 0))
    row = pl.BlockSpec((1, cols), lambda u: (0, 0))
    return pl.pallas_call(
        functools.partial(finish_kernel, length),
        grid=(users,),
        out_shape=jax.ShapeDtypeStruct((users, length, cols), jnp.bfloat16),
        in_specs=[block] * 4 + [whole] * 4 + [row] * 2,
        out_specs=pl.BlockSpec((1, length, cols), lambda u: (u, 0, 0)),
        compiler_params=pltpu.CompilerParams(vmem_limit_bytes=44 * 1024 * 1024),
        cost_estimate=pl.CostEstimate(
            flops=users * 8 * padded * cols * cols,
            bytes_accessed=5 * xo.size * 2 + 8 * cols * cols,
            transcendentals=0,
        ),
        name="finish",
    )(xo, xt, co, ct, *weights, gain, bias)


def swap(a):
    return lax.ppermute(a, "head", [(0, 1), (1, 0)])


def build_requests(owner, local_row, n_leaf, capacity):
    onehot = owner[None, :] == jnp.arange(n_leaf, dtype=jnp.int32)[:, None]
    counted = onehot.astype(jnp.int32)
    rank = jnp.sum((jnp.cumsum(counted, axis=1) - counted) * counted, axis=0)
    high, low = local_row // 64, local_row % 64
    parts = jnp.concatenate(
        [jnp.where(onehot, high[None, :], 0), jnp.where(onehot, low[None, :], 0)], axis=0
    ).astype(jnp.bfloat16)
    slots = (rank[:, None] == jnp.arange(capacity, dtype=jnp.int32)[None, :]).astype(jnp.bfloat16)
    placed = mm(parts, slots).astype(jnp.int32)
    return placed[:n_leaf] * 64 + placed[n_leaf:], owner * capacity + rank


def shards(cand_owner, cand_row, table, position, w_query, w_key, w_value, w_out, gain, shift_bias):
    users, length, _ = cand_owner.shape
    total = users * length
    cols = table.shape[1]
    n_leaf = lax.axis_size("leaf")
    head = lax.axis_index("head")
    own, other = head * cols, (1 - head) * cols
    capacity = (max(2, 2 * total // n_leaf) + 7) // 8 * 8
    padded = (length + 15) // 16 * 16

    requests, target = build_requests(
        cand_owner.reshape(total), cand_row.reshape(total), n_leaf, capacity
    )
    asked = lax.all_to_all(requests, "leaf", split_axis=0, concat_axis=0, tiled=True)
    found = table.at[asked.reshape(n_leaf * capacity)].get(mode="promise_in_bounds")
    fetched = lax.all_to_all(
        found.reshape(n_leaf, capacity, cols), "leaf", split_axis=0, concat_axis=0, tiled=True
    ).reshape(n_leaf * capacity, cols)

    def rows_of(w, start):
        return lax.dynamic_slice(w, (start, 0), (cols, cols))

    def columns_of(w, start):
        return lax.dynamic_slice(w, (0, start), (cols, cols))

    qkv = [rows_of(w, start) for w in (w_query, w_key, w_value) for start in (own, other)]
    w_out_other = swap(w_out)
    mix = [columns_of(w, start) for start in (own, other) for w in (w_out, w_out_other)]

    target = jnp.pad(target.reshape(users, length), ((0, 0), (0, padded - length)), mode="edge")
    shift = jnp.pad(position, ((0, padded - length), (0, 0)), mode="edge").astype(jnp.float32)
    part = users // SPLIT
    mine, theirs, context, context_other = [], [], [], []
    for index in range(SPLIT):
        places = target[index * part : (index + 1) * part].reshape(part * padded)
        rows = fetched.at[places].get(mode="promise_in_bounds").reshape(part, padded, cols)
        x = (rows.astype(jnp.float32) + shift[None]).astype(jnp.bfloat16)
        mine.append(x)
        theirs.append(swap(x))
    for index in range(SPLIT):
        c = attend(length, mine[index], theirs[index], qkv)
        context.append(c)
        context_other.append(swap(c))
    done = [
        finish(
            length,
            mine[index],
            theirs[index],
            context[index],
            context_other[index],
            mix,
            gain.reshape(1, cols),
            shift_bias.reshape(1, cols),
        )
        for index in range(SPLIT)
    ]
    return jnp.concatenate(done, axis=0)


def solution(mesh):
    return jax.shard_map(
        shards,
        mesh=mesh,
        in_specs=(
            P("leaf", None, None),
            P("leaf", None),
            P("leaf", "head"),
            P(None, "head"),
            P(None, "head"),
            P(None, "head"),
            P(None, "head"),
            P("head", None),
            P("head"),
            P("head"),
        ),
        out_specs=P("leaf", None, "head"),
        check_vma=False,
    )
```

```python
import functools
import math

import jax
import jax.numpy as jnp
from jax import lax
from jax.experimental import pallas as pl
from jax.experimental.pallas import tpu as pltpu
from jax.sharding import PartitionSpec as P

HEAD_DIM = 64
PAIR = 2 * HEAD_DIM
SPLIT = 2
CUTS = (0, 3, 9, 14)


def mm(a, b):
    return jnp.dot(a, b, preferred_element_type=jnp.float32)


def attend_kernel(length, xo_ref, xt_ref, qo, qt, ko, kt, vo, vt, ctx_ref):
    xo, xt = xo_ref[0], xt_ref[0]
    padded, cols = xo.shape
    scale = math.log2(math.e) / HEAD_DIM**0.5
    q = ((mm(xo, qo[...]) + mm(xt, qt[...])) * scale).astype(jnp.bfloat16)
    k = (mm(xo, ko[...]) + mm(xt, kt[...])).astype(jnp.bfloat16)
    v = (mm(xo, vo[...]) + mm(xt, vt[...])).astype(jnp.bfloat16)
    low = lax.broadcasted_iota(jnp.int32, (padded, PAIR), 1) < HEAD_DIM
    real = lax.broadcasted_iota(jnp.int32, (padded, PAIR), 0) < length
    ones = jnp.where(real, 1.0, 0.0).astype(jnp.bfloat16)
    for pair in range(cols // PAIR):
        lanes = slice(pair * PAIR, (pair + 1) * PAIR)
        qp, kp, vp = q[:, lanes], k[:, lanes], v[:, lanes]
        vx = jnp.concatenate([jnp.where(real, vp, jnp.zeros_like(vp)), ones], axis=1)
        halves = []
        for mask in (low, jnp.logical_not(low)):
            qm = jnp.where(mask, qp, jnp.zeros_like(qp))
            s = lax.dot_general(
                qm, kp, (((1,), (1,)), ((), ())), preferred_element_type=jnp.float32
            )
            e = jnp.exp2(s - jnp.max(s, axis=1, keepdims=True)).astype(jnp.bfloat16)
            o = mm(e, vx)
            halves.append(o[:, :PAIR] / o[:, PAIR:])
        ctx_ref[0, :, lanes] = jnp.where(low, halves[0], halves[1]).astype(jnp.bfloat16)


def attend(length, xo, xt, weights):
    users, padded, cols = xo.shape
    block = pl.BlockSpec((1, padded, cols), lambda u: (u, 0, 0))
    whole = pl.BlockSpec((cols, cols), lambda u: (0, 0))
    flops = users * (12 * padded * cols * cols + 8 * padded * padded * cols)
    return pl.pallas_call(
        functools.partial(attend_kernel, length),
        grid=(users,),
        out_shape=jax.ShapeDtypeStruct(xo.shape, jnp.bfloat16),
        in_specs=[block, block] + [whole] * 6,
        out_specs=block,
        compiler_params=pltpu.CompilerParams(vmem_limit_bytes=44 * 1024 * 1024),
        cost_estimate=pl.CostEstimate(
            flops=flops,
            bytes_accessed=3 * xo.size * 2 + 12 * cols * cols,
            transcendentals=users * (cols // HEAD_DIM) * padded * padded,
        ),
        name="attend",
    )(xo, xt, *weights)


def finish_kernel(length, xo_ref, xt_ref, co_ref, ct_ref, oo, to, ot, tt, gain, bias, out_ref):
    co, ct = co_ref[0], ct_ref[0]
    yo = xo_ref[0].astype(jnp.float32) + mm(co, oo[...]) + mm(ct, to[...])
    yt = xt_ref[0].astype(jnp.float32) + mm(co, ot[...]) + mm(ct, tt[...])
    width = 2 * yo.shape[1]
    mean = jnp.sum(yo + yt, axis=1, keepdims=True) / width
    var = jnp.sum(yo * yo + yt * yt, axis=1, keepdims=True) / width - mean * mean
    normed = (yo - mean) * lax.rsqrt(var + 1e-05) * gain[...] + bias[...]
    out_ref[0] = normed[:length].astype(jnp.bfloat16)


def finish(length, xo, xt, co, ct, weights, gain, bias):
    users, padded, cols = xo.shape
    block = pl.BlockSpec((1, padded, cols), lambda u: (u, 0, 0))
    whole = pl.BlockSpec((cols, cols), lambda u: (0, 0))
    row = pl.BlockSpec((1, cols), lambda u: (0, 0))
    return pl.pallas_call(
        functools.partial(finish_kernel, length),
        grid=(users,),
        out_shape=jax.ShapeDtypeStruct((users, length, cols), jnp.bfloat16),
        in_specs=[block] * 4 + [whole] * 4 + [row] * 2,
        out_specs=pl.BlockSpec((1, length, cols), lambda u: (u, 0, 0)),
        compiler_params=pltpu.CompilerParams(vmem_limit_bytes=44 * 1024 * 1024),
        cost_estimate=pl.CostEstimate(
            flops=users * 8 * padded * cols * cols,
            bytes_accessed=5 * xo.size * 2 + 8 * cols * cols,
            transcendentals=0,
        ),
        name="finish",
    )(xo, xt, co, ct, *weights, gain, bias)


def swap(a):
    return lax.ppermute(a, "head", [(0, 1), (1, 0)])


def rank_candidates(owner, n_leaf):
    onehot = owner[None, :] == jnp.arange(n_leaf, dtype=jnp.int32)[:, None]
    counted = onehot.astype(jnp.int32)
    return onehot, jnp.sum((jnp.cumsum(counted, axis=1) - counted) * counted, axis=0)


def place_requests(onehot, rank, local_row, capacity):
    n_leaf = onehot.shape[0]
    high, low = local_row // 64, local_row % 64
    parts = jnp.concatenate(
        [jnp.where(onehot, high[None, :], 0), jnp.where(onehot, low[None, :], 0)], axis=0
    ).astype(jnp.bfloat16)
    slots = (rank[:, None] == jnp.arange(capacity, dtype=jnp.int32)[None, :]).astype(jnp.bfloat16)
    placed = mm(parts, slots).astype(jnp.int32)
    return placed[:n_leaf] * 64 + placed[n_leaf:]


def shards(cand_owner, cand_row, table, position, w_query, w_key, w_value, w_out, gain, shift_bias):
    users, length, _ = cand_owner.shape
    total = users * length
    cols = table.shape[1]
    n_leaf = lax.axis_size("leaf")
    head = lax.axis_index("head")
    own, other = head * cols, (1 - head) * cols
    capacity = (max(2, 2 * total // n_leaf) + 7) // 8 * 8
    padded = (length + 15) // 16 * 16

    half = n_leaf // 2
    groups = [list(range(half)), list(range(half, n_leaf))]
    side = lax.axis_index("leaf") // half
    mirror = [(i, (i + half) % n_leaf) for i in range(n_leaf)]
    cuts = [table.shape[0] * c // 32 for c in CUTS]

    def exchange(a):
        return lax.all_to_all(
            a, "leaf", split_axis=0, concat_axis=0, tiled=True, axis_index_groups=groups
        )

    def mirrored(piece, beside):
        moved = lax.ppermute(table[cuts[piece] : cuts[piece + 1]], "leaf", mirror)
        return lax.optimization_barrier((moved, beside))

    owner = cand_owner.reshape(total)
    onehot, rank = rank_candidates(owner, n_leaf)
    far_a, rank = mirrored(0, rank)
    requests = place_requests(onehot, rank, cand_row.reshape(total), capacity)
    sides = requests.reshape(2, half, capacity)
    near = lax.dynamic_index_in_dim(sides, side, 0, keepdims=False)
    far = lax.dynamic_index_in_dim(sides, 1 - side, 0, keepdims=False)
    far_b, asked = mirrored(1, exchange(jnp.concatenate([near, far], axis=1)))

    def find(block, places):
        return block.at[places.reshape(half * capacity)].get(mode="promise_in_bounds")

    def send(found):
        return exchange(found.reshape(half, capacity, cols)).reshape(half * capacity, cols)

    far_c, found = mirrored(2, find(table, asked[:, :capacity]))
    fetched_near = send(found)
    far_d = lax.ppermute(table[cuts[3] :], "leaf", mirror)
    far_table = jnp.concatenate([far_a, far_b, far_c, far_d], axis=0)
    fetched_far = send(find(far_table, asked[:, capacity:]))

    def rows_of(w, start):
        return lax.dynamic_slice(w, (start, 0), (cols, cols))

    def columns_of(w, start):
        return lax.dynamic_slice(w, (0, start), (cols, cols))

    qkv = [rows_of(w, start) for w in (w_query, w_key, w_value) for start in (own, other)]
    fetched_near, w_out_other = lax.optimization_barrier((fetched_near, swap(w_out)))
    mix = [columns_of(w, start) for start in (own, other) for w in (w_out, w_out_other)]

    target = owner * capacity + rank
    is_near = target // (half * capacity) == side
    target = target % (half * capacity)
    is_near = jnp.pad(is_near.reshape(users, length), ((0, 0), (0, padded - length)), mode="edge")
    target = jnp.pad(target.reshape(users, length), ((0, 0), (0, padded - length)), mode="edge")
    shift = jnp.pad(position, ((0, padded - length), (0, 0)), mode="edge").astype(jnp.float32)
    part = users // SPLIT
    mine, theirs, context, context_other = [], [], [], []
    for index in range(SPLIT):
        some = slice(index * part, (index + 1) * part)
        places = target[some].reshape(part * padded)
        rows_near, rows_far = (
            f.at[places].get(mode="promise_in_bounds").reshape(part, padded, cols)
            for f in (fetched_near, fetched_far)
        )
        rows = jnp.where(is_near[some][:, :, None], rows_near, rows_far)
        x = (rows.astype(jnp.float32) + shift[None]).astype(jnp.bfloat16)
        mine.append(x)
        theirs.append(swap(x))
    for index in range(SPLIT):
        c = attend(length, mine[index], theirs[index], qkv)
        context.append(c)
        context_other.append(swap(c))
    done = [
        finish(
            length,
            mine[index],
            theirs[index],
            context[index],
            context_other[index],
            mix,
            gain.reshape(1, cols),
            shift_bias.reshape(1, cols),
        )
        for index in range(SPLIT)
    ]
    return jnp.concatenate(done, axis=0)


def solution(mesh):
    return jax.shard_map(
        shards,
        mesh=mesh,
        in_specs=(
            P("leaf", None, None),
            P("leaf", None),
            P("leaf", "head"),
            P(None, "head"),
            P(None, "head"),
            P(None, "head"),
            P(None, "head"),
            P("head", None),
            P("head"),
            P("head"),
        ),
        out_specs=P("leaf", None, "head"),
        check_vma=False,
    )
```

```python
import functools
import math

import jax
import jax.numpy as jnp
from jax import lax
from jax.experimental import pallas as pl
from jax.experimental.pallas import tpu as pltpu
from jax.sharding import PartitionSpec as P

HEAD_DIM = 64
PAIR = 2 * HEAD_DIM
SPLIT = 2
CUTS = (0, 1, 11, 19)


def mm(a, b):
    return jnp.dot(a, b, preferred_element_type=jnp.float32)


def attend_kernel(length, xo_ref, xt_ref, qo, qt, ko, kt, vo, vt, ctx_ref):
    xo, xt = xo_ref[0], xt_ref[0]
    padded, cols = xo.shape
    scale = math.log2(math.e) / HEAD_DIM**0.5
    q = ((mm(xo, qo[...]) + mm(xt, qt[...])) * scale).astype(jnp.bfloat16)
    k = (mm(xo, ko[...]) + mm(xt, kt[...])).astype(jnp.bfloat16)
    v = (mm(xo, vo[...]) + mm(xt, vt[...])).astype(jnp.bfloat16)
    low = lax.broadcasted_iota(jnp.int32, (padded, PAIR), 1) < HEAD_DIM
    real = lax.broadcasted_iota(jnp.int32, (padded, PAIR), 0) < length
    ones = jnp.where(real, 1.0, 0.0).astype(jnp.bfloat16)
    for pair in range(cols // PAIR):
        lanes = slice(pair * PAIR, (pair + 1) * PAIR)
        qp, kp, vp = q[:, lanes], k[:, lanes], v[:, lanes]
        vx = jnp.concatenate([jnp.where(real, vp, jnp.zeros_like(vp)), ones], axis=1)
        halves = []
        for mask in (low, jnp.logical_not(low)):
            qm = jnp.where(mask, qp, jnp.zeros_like(qp))
            s = lax.dot_general(
                qm, kp, (((1,), (1,)), ((), ())), preferred_element_type=jnp.float32
            )
            e = jnp.exp2(s - jnp.max(s, axis=1, keepdims=True)).astype(jnp.bfloat16)
            o = mm(e, vx)
            halves.append(o[:, :PAIR] / o[:, PAIR:])
        ctx_ref[0, :, lanes] = jnp.where(low, halves[0], halves[1]).astype(jnp.bfloat16)


def attend(length, xo, xt, weights):
    users, padded, cols = xo.shape
    block = pl.BlockSpec((1, padded, cols), lambda u: (u, 0, 0))
    whole = pl.BlockSpec((cols, cols), lambda u: (0, 0))
    flops = users * (12 * padded * cols * cols + 8 * padded * padded * cols)
    return pl.pallas_call(
        functools.partial(attend_kernel, length),
        grid=(users,),
        out_shape=jax.ShapeDtypeStruct(xo.shape, jnp.bfloat16),
        in_specs=[block, block] + [whole] * 6,
        out_specs=block,
        compiler_params=pltpu.CompilerParams(vmem_limit_bytes=44 * 1024 * 1024),
        cost_estimate=pl.CostEstimate(
            flops=flops,
            bytes_accessed=3 * xo.size * 2 + 12 * cols * cols,
            transcendentals=users * (cols // HEAD_DIM) * padded * padded,
        ),
        name="attend",
    )(xo, xt, *weights)


def finish_kernel(length, xo_ref, xt_ref, co_ref, ct_ref, oo, to, ot, tt, gain, bias, out_ref):
    co, ct = co_ref[0], ct_ref[0]
    yo = xo_ref[0].astype(jnp.float32) + mm(co, oo[...]) + mm(ct, to[...])
    yt = xt_ref[0].astype(jnp.float32) + mm(co, ot[...]) + mm(ct, tt[...])
    width = 2 * yo.shape[1]
    mean = jnp.sum(yo + yt, axis=1, keepdims=True) / width
    var = jnp.sum(yo * yo + yt * yt, axis=1, keepdims=True) / width - mean * mean
    normed = (yo - mean) * lax.rsqrt(var + 1e-05) * gain[...] + bias[...]
    out_ref[0] = normed[:length].astype(jnp.bfloat16)


def finish(length, xo, xt, co, ct, weights, gain, bias):
    users, padded, cols = xo.shape
    block = pl.BlockSpec((1, padded, cols), lambda u: (u, 0, 0))
    whole = pl.BlockSpec((cols, cols), lambda u: (0, 0))
    row = pl.BlockSpec((1, cols), lambda u: (0, 0))
    return pl.pallas_call(
        functools.partial(finish_kernel, length),
        grid=(users,),
        out_shape=jax.ShapeDtypeStruct((users, length, cols), jnp.bfloat16),
        in_specs=[block] * 4 + [whole] * 4 + [row] * 2,
        out_specs=pl.BlockSpec((1, length, cols), lambda u: (u, 0, 0)),
        compiler_params=pltpu.CompilerParams(vmem_limit_bytes=44 * 1024 * 1024),
        cost_estimate=pl.CostEstimate(
            flops=users * 8 * padded * cols * cols,
            bytes_accessed=5 * xo.size * 2 + 8 * cols * cols,
            transcendentals=0,
        ),
        name="finish",
    )(xo, xt, co, ct, *weights, gain, bias)


def swap(a):
    return lax.ppermute(a, "head", [(0, 1), (1, 0)])


def rank_candidates(owner, n_leaf):
    onehot = owner[None, :] == jnp.arange(n_leaf, dtype=jnp.int32)[:, None]
    counted = onehot.astype(jnp.int32)
    return onehot, jnp.sum((jnp.cumsum(counted, axis=1) - counted) * counted, axis=0)


def place_requests(onehot, rank, local_row, capacity):
    n_leaf = onehot.shape[0]
    high, low = local_row // 64, local_row % 64
    parts = jnp.concatenate(
        [jnp.where(onehot, high[None, :], 0), jnp.where(onehot, low[None, :], 0)], axis=0
    ).astype(jnp.bfloat16)
    slots = (rank[:, None] == jnp.arange(capacity, dtype=jnp.int32)[None, :]).astype(jnp.bfloat16)
    placed = mm(parts, slots).astype(jnp.int32)
    return placed[:n_leaf] * 64 + placed[n_leaf:]


def shards(cand_owner, cand_row, table, position, w_query, w_key, w_value, w_out, gain, shift_bias):
    users, length, _ = cand_owner.shape
    total = users * length
    cols = table.shape[1]
    n_leaf = lax.axis_size("leaf")
    head = lax.axis_index("head")
    own, other = head * cols, (1 - head) * cols
    capacity = (max(2, 2 * total // n_leaf) + 7) // 8 * 8
    padded = (length + 15) // 16 * 16

    half = n_leaf // 2
    groups = [list(range(half)), list(range(half, n_leaf))]
    side = lax.axis_index("leaf") // half
    mirror = [(i, (i + half) % n_leaf) for i in range(n_leaf)]
    cuts = [table.shape[0] * c // 32 for c in CUTS]

    def exchange(a):
        return lax.all_to_all(
            a, "leaf", split_axis=0, concat_axis=0, tiled=True, axis_index_groups=groups
        )

    def mirrored(piece, beside):
        moved = lax.ppermute(table[cuts[piece] : cuts[piece + 1]], "leaf", mirror)
        return lax.optimization_barrier((moved, beside))

    owner = cand_owner.reshape(total)
    onehot, rank = rank_candidates(owner, n_leaf)
    far_a, rank = mirrored(0, rank)
    requests = place_requests(onehot, rank, cand_row.reshape(total), capacity)
    sides = requests.reshape(2, half, capacity)
    near = lax.dynamic_index_in_dim(sides, side, 0, keepdims=False)
    far = lax.dynamic_index_in_dim(sides, 1 - side, 0, keepdims=False)
    far_b, asked = mirrored(1, exchange(jnp.concatenate([near, far], axis=1)))

    def find(block, places):
        return block.at[places.reshape(half * capacity)].get(mode="promise_in_bounds")

    def send(found):
        return exchange(found.reshape(half, capacity, cols)).reshape(half * capacity, cols)

    far_c, found = mirrored(2, find(table, asked[:, :capacity]))
    fetched_near = send(found)
    far_d = lax.ppermute(table[cuts[3] :], "leaf", mirror)
    far_table = jnp.concatenate([far_a, far_b, far_c, far_d], axis=0)
    fetched_far = send(find(far_table, asked[:, capacity:]))

    def rows_of(w, start):
        return lax.dynamic_slice(w, (start, 0), (cols, cols))

    def columns_of(w, start):
        return lax.dynamic_slice(w, (0, start), (cols, cols))

    qkv = [rows_of(w, start) for w in (w_query, w_key, w_value) for start in (own, other)]
    fetched_near, w_out_other = lax.optimization_barrier((fetched_near, swap(w_out)))
    mix = [columns_of(w, start) for start in (own, other) for w in (w_out, w_out_other)]

    target = owner * capacity + rank
    is_near = target // (half * capacity) == side
    target = target % (half * capacity)
    is_near = jnp.pad(is_near.reshape(users, length), ((0, 0), (0, padded - length)), mode="edge")
    target = jnp.pad(target.reshape(users, length), ((0, 0), (0, padded - length)), mode="edge")
    shift = jnp.pad(position, ((0, padded - length), (0, 0)), mode="edge").astype(jnp.float32)
    part = users // SPLIT
    mine, theirs, context, context_other = [], [], [], []
    for index in range(SPLIT):
        some = slice(index * part, (index + 1) * part)
        places = target[some].reshape(part * padded)
        rows_near, rows_far = (
            f.at[places].get(mode="promise_in_bounds").reshape(part, padded, cols)
            for f in (fetched_near, fetched_far)
        )
        rows = jnp.where(is_near[some][:, :, None], rows_near, rows_far)
        x = (rows.astype(jnp.float32) + shift[None]).astype(jnp.bfloat16)
        mine.append(x)
        theirs.append(swap(x))
    for index in range(SPLIT):
        c = attend(length, mine[index], theirs[index], qkv)
        context.append(c)
        context_other.append(swap(c))
    done = [
        finish(
            length,
            mine[index],
            theirs[index],
            context[index],
            context_other[index],
            mix,
            gain.reshape(1, cols),
            shift_bias.reshape(1, cols),
        )
        for index in range(SPLIT)
    ]
    return jnp.concatenate(done, axis=0)


def solution(mesh):
    return jax.shard_map(
        shards,
        mesh=mesh,
        in_specs=(
            P("leaf", None, None),
            P("leaf", None),
            P("leaf", "head"),
            P(None, "head"),
            P(None, "head"),
            P(None, "head"),
            P(None, "head"),
            P("head", None),
            P("head"),
            P("head"),
        ),
        out_specs=P("leaf", None, "head"),
        check_vma=False,
    )
```

```python
import functools
import math

import jax
import jax.numpy as jnp
from jax import lax
from jax.experimental import pallas as pl
from jax.experimental.pallas import tpu as pltpu
from jax.sharding import PartitionSpec as P

HEAD_DIM = 64
PAIR = 2 * HEAD_DIM
SPLIT = 2


def mm(a, b):
    return jnp.dot(a, b, preferred_element_type=jnp.float32)


def attend_kernel(length, xo_ref, xt_ref, qo, qt, ko, kt, vo, vt, ctx_ref):
    xo, xt = xo_ref[0], xt_ref[0]
    padded, cols = xo.shape
    scale = math.log2(math.e) / HEAD_DIM**0.5
    q = ((mm(xo, qo[...]) + mm(xt, qt[...])) * scale).astype(jnp.bfloat16)
    k = (mm(xo, ko[...]) + mm(xt, kt[...])).astype(jnp.bfloat16)
    v = (mm(xo, vo[...]) + mm(xt, vt[...])).astype(jnp.bfloat16)
    low = lax.broadcasted_iota(jnp.int32, (padded, PAIR), 1) < HEAD_DIM
    real = lax.broadcasted_iota(jnp.int32, (padded, PAIR), 0) < length
    ones = jnp.where(real, 1.0, 0.0).astype(jnp.bfloat16)
    for pair in range(cols // PAIR):
        lanes = slice(pair * PAIR, (pair + 1) * PAIR)
        qp, kp, vp = q[:, lanes], k[:, lanes], v[:, lanes]
        vx = jnp.concatenate([jnp.where(real, vp, jnp.zeros_like(vp)), ones], axis=1)
        halves = []
        for mask in (low, jnp.logical_not(low)):
            qm = jnp.where(mask, qp, jnp.zeros_like(qp))
            s = lax.dot_general(
                qm, kp, (((1,), (1,)), ((), ())), preferred_element_type=jnp.float32
            )
            e = jnp.exp2(s - jnp.max(s, axis=1, keepdims=True)).astype(jnp.bfloat16)
            o = mm(e, vx)
            halves.append(o[:, :PAIR] / o[:, PAIR:])
        ctx_ref[0, :, lanes] = jnp.where(low, halves[0], halves[1]).astype(jnp.bfloat16)


def attend(length, xo, xt, weights):
    users, padded, cols = xo.shape
    block = pl.BlockSpec((1, padded, cols), lambda u: (u, 0, 0))
    whole = pl.BlockSpec((cols, cols), lambda u: (0, 0))
    flops = users * (12 * padded * cols * cols + 8 * padded * padded * cols)
    return pl.pallas_call(
        functools.partial(attend_kernel, length),
        grid=(users,),
        out_shape=jax.ShapeDtypeStruct(xo.shape, jnp.bfloat16),
        in_specs=[block, block] + [whole] * 6,
        out_specs=block,
        compiler_params=pltpu.CompilerParams(vmem_limit_bytes=44 * 1024 * 1024),
        cost_estimate=pl.CostEstimate(
            flops=flops,
            bytes_accessed=3 * xo.size * 2 + 12 * cols * cols,
            transcendentals=users * (cols // HEAD_DIM) * padded * padded,
        ),
        name="attend",
    )(xo, xt, *weights)


def finish_kernel(length, xo_ref, xt_ref, co_ref, ct_ref, oo, to, ot, tt, gain, bias, out_ref):
    co, ct = co_ref[0], ct_ref[0]
    yo = xo_ref[0].astype(jnp.float32) + mm(co, oo[...]) + mm(ct, to[...])
    yt = xt_ref[0].astype(jnp.float32) + mm(co, ot[...]) + mm(ct, tt[...])
    width = 2 * yo.shape[1]
    mean = jnp.sum(yo + yt, axis=1, keepdims=True) / width
    var = jnp.sum(yo * yo + yt * yt, axis=1, keepdims=True) / width - mean * mean
    normed = (yo - mean) * lax.rsqrt(var + 1e-05) * gain[...] + bias[...]
    out_ref[0] = normed[:length].astype(jnp.bfloat16)


def finish(length, xo, xt, co, ct, weights, gain, bias):
    users, padded, cols = xo.shape
    block = pl.BlockSpec((1, padded, cols), lambda u: (u, 0, 0))
    whole = pl.BlockSpec((cols, cols), lambda u: (0, 0))
    row = pl.BlockSpec((1, cols), lambda u: (0, 0))
    return pl.pallas_call(
        functools.partial(finish_kernel, length),
        grid=(users,),
        out_shape=jax.ShapeDtypeStruct((users, length, cols), jnp.bfloat16),
        in_specs=[block] * 4 + [whole] * 4 + [row] * 2,
        out_specs=pl.BlockSpec((1, length, cols), lambda u: (u, 0, 0)),
        compiler_params=pltpu.CompilerParams(vmem_limit_bytes=44 * 1024 * 1024),
        cost_estimate=pl.CostEstimate(
            flops=users * 8 * padded * cols * cols,
            bytes_accessed=5 * xo.size * 2 + 8 * cols * cols,
            transcendentals=0,
        ),
        name="finish",
    )(xo, xt, co, ct, *weights, gain, bias)


def swap(a):
    return lax.ppermute(a, "head", [(0, 1), (1, 0)])


def rank_candidates(owner, n_leaf):
    onehot = owner[None, :] == jnp.arange(n_leaf, dtype=jnp.int32)[:, None]
    counted = onehot.astype(jnp.int32)
    return onehot, jnp.sum((jnp.cumsum(counted, axis=1) - counted) * counted, axis=0)


def place_requests(onehot, rank, local_row, capacity):
    n_leaf = onehot.shape[0]
    high, low = local_row // 64, local_row % 64
    parts = jnp.concatenate(
        [jnp.where(onehot, high[None, :], 0), jnp.where(onehot, low[None, :], 0)], axis=0
    ).astype(jnp.bfloat16)
    slots = (rank[:, None] == jnp.arange(capacity, dtype=jnp.int32)[None, :]).astype(jnp.bfloat16)
    placed = mm(parts, slots).astype(jnp.int32)
    return placed[:n_leaf] * 64 + placed[n_leaf:]


def shards(cand_owner, cand_row, table, position, w_query, w_key, w_value, w_out, gain, shift_bias):
    users, length, _ = cand_owner.shape
    total = users * length
    cols = table.shape[1]
    n_leaf = lax.axis_size("leaf")
    head = lax.axis_index("head")
    own, other = head * cols, (1 - head) * cols
    capacity = (max(2, 2 * total // n_leaf) + 7) // 8 * 8
    padded = (length + 15) // 16 * 16

    half = n_leaf // 2
    groups = [list(range(half)), list(range(half, n_leaf))]
    side = lax.axis_index("leaf") // half
    mirror = [(i, (i + half) % n_leaf) for i in range(n_leaf)]

    def exchange(a):
        return lax.all_to_all(
            a, "leaf", split_axis=0, concat_axis=0, tiled=True, axis_index_groups=groups
        )

    far_table = lax.ppermute(table, "leaf", mirror)
    owner = cand_owner.reshape(total)
    onehot, rank = rank_candidates(owner, n_leaf)
    requests = place_requests(onehot, rank, cand_row.reshape(total), capacity)
    sides = requests.reshape(2, half, capacity)
    near = lax.dynamic_index_in_dim(sides, side, 0, keepdims=False)
    far = lax.dynamic_index_in_dim(sides, 1 - side, 0, keepdims=False)
    asked = exchange(jnp.concatenate([near, far], axis=1))

    def find(block, places):
        return block.at[places.reshape(half * capacity)].get(mode="promise_in_bounds")

    def send(found):
        return exchange(found.reshape(half, capacity, cols)).reshape(half * capacity, cols)

    far_table, found = lax.optimization_barrier((far_table, find(table, asked[:, :capacity])))
    fetched_near = send(found)
    fetched_far = send(find(far_table, asked[:, capacity:]))

    def rows_of(w, start):
        return lax.dynamic_slice(w, (start, 0), (cols, cols))

    def columns_of(w, start):
        return lax.dynamic_slice(w, (0, start), (cols, cols))

    qkv = [rows_of(w, start) for w in (w_query, w_key, w_value) for start in (own, other)]
    fetched_near, w_out_other = lax.optimization_barrier((fetched_near, swap(w_out)))
    mix = [columns_of(w, start) for start in (own, other) for w in (w_out, w_out_other)]

    target = owner * capacity + rank
    is_near = target // (half * capacity) == side
    target = target % (half * capacity)
    is_near = jnp.pad(is_near.reshape(users, length), ((0, 0), (0, padded - length)), mode="edge")
    target = jnp.pad(target.reshape(users, length), ((0, 0), (0, padded - length)), mode="edge")
    shift = jnp.pad(position, ((0, padded - length), (0, 0)), mode="edge").astype(jnp.float32)
    part = users // SPLIT
    mine, theirs, context, context_other = [], [], [], []
    places = target.reshape(users * padded)

    def pick(fetched, some):
        picked = fetched.at[some].get(mode="promise_in_bounds")
        return picked.reshape(-1, padded, cols)

    fetched_far, every_near = lax.optimization_barrier((fetched_far, pick(fetched_near, places)))
    for index in range(SPLIT):
        some = slice(index * part, (index + 1) * part)
        rows_far = pick(fetched_far, target[some].reshape(part * padded))
        rows = jnp.where(is_near[some][:, :, None], every_near[some], rows_far)
        x = (rows.astype(jnp.float32) + shift[None]).astype(jnp.bfloat16)
        mine.append(x)
        theirs.append(swap(x))
    for index in range(SPLIT):
        c = attend(length, mine[index], theirs[index], qkv)
        context.append(c)
        context_other.append(swap(c))
    done = [
        finish(
            length,
            mine[index],
            theirs[index],
            context[index],
            context_other[index],
            mix,
            gain.reshape(1, cols),
            shift_bias.reshape(1, cols),
        )
        for index in range(SPLIT)
    ]
    return jnp.concatenate(done, axis=0)


def solution(mesh):
    return jax.shard_map(
        shards,
        mesh=mesh,
        in_specs=(
            P("leaf", None, None),
            P("leaf", None),
            P("leaf", "head"),
            P(None, "head"),
            P(None, "head"),
            P(None, "head"),
            P(None, "head"),
            P("head", None),
            P("head"),
            P("head"),
        ),
        out_specs=P("leaf", None, "head"),
        check_vma=False,
    )
```
